256 devices in a mesh: store: 32 (over z, y), pb: 8 (over x, core).
Axes of the slice: x: 4, y: 4, z: 8, core: 2. Of those that a mesh axis runs over, the one named last changes fastest.
Arguments:
- stored_hidden: bfloat16 [640, 32, 4096], P('store')
- targets: int32 [640, 32], P('store'), may hold values from 0 to 5119
- pick: int32 [512], P('store'), may hold values from 0 to 19, as said below
- dest: int32 [512], P('store'), may hold values from 0 to 31, as said below
- norm_gain: float32 [4096], replicated, may hold values from 0.1 to 1.9
- head: bfloat16 [4096, 5120], P(None, 'pb')
- proj_in: bfloat16 [4096, 64], replicated, may hold values from -0.09375 to 0.09375
- proj_out: bfloat16 [5120, 128], P('pb'), may hold values from -6 to 6
- query_grads: bfloat16 [4096, 8192], P(('store', 'pb')), may hold values from -0.011962891 to 0.011962891
Outputs:
- shortlist: float32 [4096, 2], P(('store', 'pb'))
The draws below stay inside these ranges and needn't reach their ends.
Inputs may be any that keep to these rules, and one draw needn't show every extreme that they name: `pick`: within one storage shard's 16 candidates the example numbers are distinct. `dest`: one storage shard sends at most 2 candidates to one query block; every query block receives at least 2 candidates.
All inputs are finite; a program needn't handle non-finite values.
Results may differ from the reference program's by a relative error of at most 0.003.
Values may be sent and summed in bfloat16 or wider, within the bound.
A program may use at most 128 MiB of HBM per device.

```python
import jax
import jax.numpy as jnp
from jax import lax

D = 4096
V_DEV = 640
PROJ_IN = 64
PROJ_OUT = 128
T_EX = 32
S_EX = 20
C_SRC = 16
CAP = 2
K_TOP = 2
VOCAB = 5120
Q_BLOCK = 128
QUERIES = 4096
STORED = 640
CANDS = 512
N_STORE = 32
N_PB = 8


def common_direction(key):
    return jnp.where(jax.random.bernoulli(key, 0.5, (D,)), 1.0, -1.0).astype(jnp.float32)


def draw_stored_hidden(key, part):
    direction = common_direction(key)
    key = jax.random.fold_in(key, 11)
    key_noise, key_scale, key_pull, key_strong, key_kind = jax.random.split(key, 5)
    weak = jax.random.uniform(key_pull, (STORED, 1, 1), jnp.float32, 0.0, 0.12)
    strong = jax.random.uniform(key_strong, (STORED, 1, 1), jnp.float32, 1.0, 4.0)
    kind = jax.random.bernoulli(key_kind, 0.25, (STORED, 1, 1))
    strength = jnp.where(kind, strong, weak)
    noise = jax.random.normal(key_noise, (STORED, T_EX, D), jnp.float32)
    spread = jax.random.uniform(key_scale, (STORED, T_EX, 1), jnp.float32, -0.7, 1.4)
    noise = noise * jnp.exp(spread)
    value = noise + strength * direction[None, None, :]
    return value.astype(jnp.bfloat16)


def draw_head(key, part):
    direction = common_direction(key)
    key = jax.random.fold_in(key, 13)
    column = jnp.arange(VOCAB)
    position = column.astype(jnp.float32)
    rise = (3.0 + position / VOCAB) * D ** (-0.5)
    base = jax.random.normal(key, (D, VOCAB), jnp.float32) * rise[None, :]
    within = column % V_DEV
    shard = (column // V_DEV).astype(jnp.float32)
    lower = 1.0 - 0.1 * shard / N_PB
    strength = jnp.where(within == 0, 240.0, 238.0) * lower / D
    aligned = direction[:, None] * strength[None, :]
    base = jnp.where(within[None, :] < 2, aligned, base)
    return base.astype(jnp.bfloat16)


def draw_pick(key, part):
    key = jax.random.fold_in(key, 17)
    raw = jax.random.randint(key, (N_STORE, S_EX), 0, 65536) * S_EX + jnp.arange(S_EX)[None, :]
    order = jnp.argsort(raw, axis=1)[:, :C_SRC]
    return order.reshape(-1).astype(jnp.int32)


def draw_dest(key, part):
    key = jax.random.fold_in(key, 19)
    key_hot, key_shift, key_pop, key_rank = jax.random.split(key, 4)
    per_source = C_SRC // CAP
    hot = jax.random.randint(key_hot, (), 0, N_STORE)
    shift = jax.random.randint(key_shift, (), 0, N_STORE)
    popular = 2 ** jax.random.randint(key_pop, (N_STORE,), 0, 6)
    sources = jnp.arange(N_STORE)
    places = jnp.arange(N_STORE)
    own = (sources + shift) % N_STORE
    raw = jax.random.randint(key_rank, (N_STORE, N_STORE), 0, 1024) * popular[None, :]
    score = raw * N_STORE + places[None, :]
    score = jnp.where(places[None, :] == hot, 2 ** 30, score)
    score = jnp.where(places[None, :] == own[:, None], -1, score)
    chosen = lax.top_k(score, per_source - 1)[1]
    picked = jnp.concatenate([own[:, None], chosen], axis=1)
    return jnp.repeat(picked, CAP, axis=1).reshape(-1).astype(jnp.int32)


def set_ends(drawn, own_key, low, high):
    longest = drawn.shape.index(max(drawn.shape))
    spots = []
    for shift in (0, 1):
        where = [jax.random.randint(jax.random.fold_in(own_key, axis), (), 0, length) for axis, length in enumerate(drawn.shape)]
        where[longest] = (where[longest] + shift) % drawn.shape[longest]
        spots.append(tuple(where))
    return drawn.at[spots[0]].set(low).at[spots[1]].set(high)


def shard_levels(rng, shape, pieces, least, high):
    def one(axis_at, shards_of):
        steps = jax.random.uniform(jax.random.fold_in(jax.random.fold_in(rng, 6), axis_at), (shards_of,), jnp.float32, least / len(pieces), high / len(pieces))
        return jnp.repeat(jnp.exp(steps), shape[axis_at] // shards_of).reshape((-1,) + (1,) * (len(shape) - axis_at - 1))

    level = one(*pieces[0])
    for cut in pieces[1:]:
        level = level * one(*cut)
    return level


def normal_values(stream_key, extent, scale, most, shards=(), dtype=jnp.bfloat16):
    array = scale * jax.random.normal(stream_key, extent, jnp.float32)
    if shards:
        array = array * shard_levels(stream_key, extent, shards, -0.22, 0.18)
    return jnp.clip(array, -most, most).astype(dtype)


def setup_inputs(seed: int = 0) -> dict:
    streams_of = jax.random.split(jax.random.key(seed), 10)
    stored_hidden = draw_stored_hidden(jax.random.fold_in(streams_of[9], 71), 0)
    targets = set_ends(jax.random.randint(streams_of[1], (STORED, T_EX), 0, VOCAB), jax.random.fold_in(streams_of[1], 1), 0, VOCAB - 1).astype(jnp.int32)
    pick = draw_pick(jax.random.fold_in(streams_of[9], 71), 0)
    dest = draw_dest(jax.random.fold_in(streams_of[9], 71), 0)
    norm_gain = jnp.clip(1.0 + 0.18 * jax.random.normal(streams_of[4], (D,), jnp.float32), 0.1, 1.9)
    head = draw_head(jax.random.fold_in(streams_of[9], 71), 0)
    proj_in = normal_values(streams_of[6], (D, PROJ_IN), D ** -0.5, 0.09375)
    proj_out = normal_values(streams_of[7], (VOCAB, PROJ_OUT), 1.0, 6.0, ((0, 8),))
    query_grads = normal_values(streams_of[8], (QUERIES, PROJ_IN * PROJ_OUT), 0.002, 0.011962891, ((0, 256),))
    return dict(stored_hidden=stored_hidden, targets=targets, pick=pick, dest=dest, norm_gain=norm_gain, head=head, proj_in=proj_in, proj_out=proj_out, query_grads=query_grads)


def candidate_grads(ids, stored_hidden, targets, norm_gain, head, proj_in, proj_out):
    rows = jnp.take(stored_hidden, ids, axis=0).reshape(-1, D)
    wanted = jnp.take(targets, ids, axis=0).reshape(-1)
    wide = rows.astype(jnp.float32)
    scale = lax.rsqrt(lax.optimization_barrier(jnp.mean(wide * wide, axis=1)) + 1e-05)
    normed = (wide * scale[:, None] * norm_gain[None, :]).astype(jnp.bfloat16)
    logits = jnp.dot(normed, head, preferred_element_type=jnp.float32)
    top = lax.optimization_barrier(jnp.max(logits, axis=1))
    expo = jnp.exp(logits - top[:, None])
    prob = expo / lax.optimization_barrier(jnp.sum(expo, axis=1))[:, None]
    hit = (jnp.arange(VOCAB)[None, :] == wanted[:, None]).astype(jnp.float32)
    delta = (prob - hit).astype(jnp.bfloat16)
    outer_side = jnp.dot(delta, proj_out, preferred_element_type=jnp.float32)
    inner_side = jnp.dot(normed, proj_in, preferred_element_type=jnp.float32)
    grads = jnp.einsum('etk,etm->ekm', inner_side.reshape(C_SRC, T_EX, PROJ_IN), outer_side.reshape(C_SRC, T_EX, PROJ_OUT), precision=lax.Precision.HIGHEST)
    return grads.reshape(C_SRC, PROJ_IN * PROJ_OUT).astype(jnp.bfloat16)

def reference(stored_hidden, targets, pick, dest, norm_gain, head, proj_in, proj_out, query_grads):
    source = (jnp.arange(CANDS) // C_SRC).astype(jnp.int32)
    example = (source * S_EX + pick).astype(jnp.int32)

    def per_block(ids):
        return candidate_grads(ids, stored_hidden, targets, norm_gain, head, proj_in, proj_out)
    grads = lax.map(per_block, example.reshape(N_STORE, C_SRC)).reshape(CANDS, PROJ_IN * PROJ_OUT)
    blocks = query_grads.reshape(N_STORE, Q_BLOCK, PROJ_IN * PROJ_OUT)

    def one_block(inputs):
        queries, device = inputs
        scores = jnp.dot(queries, grads.T, preferred_element_type=jnp.float32)
        masked = jnp.where(dest[None, :] == device, scores, jnp.float32(-1e+30))
        return lax.top_k(masked, K_TOP)[0]
    shortlist = lax.map(one_block, (blocks, jnp.arange(N_STORE).astype(jnp.int32)))
    return shortlist.reshape(QUERIES, K_TOP)
```

```python
import functools

import jax
import jax.numpy as jnp
from jax import lax
from jax.experimental import pallas as pl
from jax.experimental.pallas import tpu as pltpu
from jax.sharding import PartitionSpec as P

CAP = 2
K_TOP = 2
CHUNKS = 2
MESH = pl.DeviceIdType.MESH
F32 = jnp.float32
BF16 = jnp.bfloat16
NT = (((1,), (1,)), ((), ()))
TN = (((0,), (0,)), ((), ()))


def kernel(
    n_store, n_pb,
    pick, dest, hid, tgt, gain, head, pin, pout, query,
    out,
    hid_v, tgt_v, gain_v, wide_w, pin_v, pout_v, query_v,
    normed, logits, inner_v, mask_v, dead_v,
    q_rows, q_mid, q_send, q_recv,
    hit_send, hit_recv, u_send, u_recv, g_send, g_recv, g_rows, s_send, s_recv,
    load_sem, hid_sem, head_sem, send_sem, recv_sem,
):
    examples, tokens, width = hid.shape
    cands = pick.shape[0]
    total_tok = cands * tokens
    v_dev = head.shape[1]
    k_in = pin.shape[1]
    m_out = pout.shape[1]
    m_loc = m_out // n_pb
    half = m_loc // 2
    per_query = query.shape[0]
    me_s = lax.axis_index("store")
    me_p = lax.axis_index("pb")

    def pb_peer(i):
        return lax.rem(me_p + i, n_pb)

    def store_peer(i):
        return lax.rem(me_s + i, n_store)

    small = [
        pltpu.make_async_copy(src, dst, load_sem.at[i])
        for i, (src, dst) in enumerate(
            [(gain, gain_v), (tgt, tgt_v), (pout, pout_v), (pin, pin_v), (query, query_v)]
        )
    ]
    gain_load, tgt_load, pout_load, pin_load, query_load = small
    cuts = list(range(0, v_dev, 256)) + [v_dev]
    head_loads = [
        pltpu.make_async_copy(
            head.at[:, lo:hi], wide_w.at[:, lo:hi], head_sem.at[i]
        )
        for i, (lo, hi) in enumerate(zip(cuts[:-1], cuts[1:]))
    ]

    def hid_load(e):
        return pltpu.make_async_copy(hid.at[e], hid_v.at[e], hid_sem.at[e])

    gain_load.start()

    @pl.loop(0, examples)
    def _(e):
        hid_load(e).start()

    tgt_load.start()
    pout_load.start()
    pin_load.start()
    for load in head_loads:
        load.start()
    query_load.start()

    barrier = pltpu.get_barrier_semaphore()
    for i in range(1, n_pb):
        pl.semaphore_signal(barrier, inc=1, device_id={"pb": pb_peer(i)}, device_id_type=MESH)

    @pl.loop(1, n_store)
    def _(i):
        pl.semaphore_signal(
            barrier, inc=1, device_id={"store": store_peer(i)}, device_id_type=MESH
        )

    gain_load.wait()
    rows = 16

    @pl.loop(0, examples)
    def _(e):
        hid_load(e).wait()
        for r in range(0, tokens, rows):
            wide = hid_v[e, r:r + rows, :].astype(F32)
            scale = lax.rsqrt(jnp.mean(wide * wide, axis=1, keepdims=True) + 1e-05)
            wide = hid_v[e, r:r + rows, :].astype(F32)
            normed[e, r:r + rows, :] = (wide * scale * gain_v[...]).astype(BF16)

    pin_load.wait()
    wide_w[:, v_dev:v_dev + k_in] = pin_v[...]
    tgt_load.wait()
    pout_load.wait()
    picks = [pick[c] for c in range(cands)]

    wanted = jnp.concatenate([tgt_v[pl.ds(p, 1), :] for p in picks], axis=1)
    column = lax.broadcasted_iota(jnp.int32, (v_dev, total_tok), 0) + me_p * v_dev
    hit = jnp.where(column == wanted, 1.0, 0.0).astype(BF16)
    hit_rows = lax.dot_general(pout_v[...], hit, TN, preferred_element_type=F32)
    hit_send[...] = hit_rows.astype(BF16).reshape(n_pb, m_loc, total_tok)

    pl.semaphore_wait(barrier, n_pb - 1 + n_store - 1)

    def pb_copy(i, src, dst, kind):
        return pltpu.make_async_remote_copy(
            src_ref=src, dst_ref=dst, send_sem=send_sem.at[kind], recv_sem=recv_sem.at[kind],
            device_id={"pb": pb_peer(i)}, device_id_type=MESH,
        )

    sent = []
    for i in range(1, n_pb):
        copy = pb_copy(i, hit_send.at[pb_peer(i)], hit_recv.at[me_p], 0)
        copy.start()
        sent.append(copy)
    hit_recv[me_p] = hit_send[me_p]

    part_c = cands // CHUNKS
    part_t = part_c * tokens
    cuts = cuts[:-1] + [v_dev + k_in]
    for chunk in range(CHUNKS):
        lo_t = chunk * part_t
        lhs = [normed[p] for p in picks[chunk * part_c:(chunk + 1) * part_c]]
        lhs = jnp.concatenate(lhs, axis=0)
        for n, (lo, hi) in enumerate(zip(cuts[:-1], cuts[1:])):
            if chunk == 0:
                head_loads[n].wait()
            logits[lo_t:lo_t + part_t, lo:hi] = jnp.dot(
                lhs, wide_w[:, lo:hi], preferred_element_type=F32
            )
        local = logits[lo_t:lo_t + part_t, :v_dev]
        top = jnp.max(local, axis=1, keepdims=True)
        expo = jnp.exp(local - top)
        total = jnp.sum(expo, axis=1, keepdims=True)
        part = jnp.dot(expo.astype(BF16), pout_v[...], preferred_element_type=F32)
        lane = lax.broadcasted_iota(jnp.int32, (part_t, 128), 1)
        stats = jnp.where(lane == 0, top, total)
        part_rows = part.T
        stat_rows = stats.T[0:8]
        for p in range(n_pb):
            u_send[chunk, p, 0:m_loc, :] = part_rows[p * m_loc:(p + 1) * m_loc]
            u_send[chunk, p, m_loc:m_loc + 8, :] = stat_rows
        for i in range(1, n_pb):
            copy = pb_copy(i, u_send.at[chunk, pb_peer(i)], u_recv.at[chunk, me_p], 1 + chunk)
            copy.start()
            sent.append(copy)
        u_recv[chunk, me_p] = u_send[chunk, me_p]

    query_load.wait()
    for k in range(k_in):
        q_rows[k * per_query:(k + 1) * per_query, :] = query_v[
            :, k * m_out:(k + 1) * m_out
        ].astype(F32)
    low = lax.broadcasted_iota(jnp.int32, (half, 2 * k_in), 1) < k_in
    for q in range(per_query):
        square = q_rows[pl.ds(q, k_in, stride=per_query), :]
        turned = jnp.concatenate([square, square], axis=0).T
        for p in range(n_pb):
            first = turned[p * m_loc:p * m_loc + half]
            second = turned[p * m_loc + half:(p + 1) * m_loc]
            q_mid[pl.ds(p * half * per_query + q, half, stride=per_query), :] = jnp.where(
                low, first, second
            )
    q_send[...] = q_mid[...].astype(BF16).reshape(q_send.shape)
    q_kind = 1 + CHUNKS
    for i in range(1, n_pb):
        copy = pb_copy(i, q_send.at[pb_peer(i)], q_recv.at[me_p], q_kind)
        copy.start()
        sent.append(copy)
    q_recv[me_p] = q_send[me_p]

    dests = [dest[c] for c in range(cands)]
    ranks = []
    for c in range(cands):
        rank = jnp.int32(0)
        for d in dests[:c]:
            rank = rank + (d == dests[c]).astype(jnp.int32)
        ranks.append(rank)
    block_of = jnp.concatenate(
        [jnp.full((1, tokens), d, jnp.int32) for d in dests], axis=1
    )
    grid_b = lax.broadcasted_iota(jnp.int32, (n_store * m_loc, total_tok), 0) // m_loc
    mask_v[...] = jnp.where(grid_b == block_of, 1.0, 0.0).astype(BF16)
    rank_of = jnp.concatenate([jnp.full((tokens, 2 * k_in), r, jnp.int32) for r in ranks], axis=0)
    inner = logits[:, v_dev:v_dev + k_in]
    inner = jnp.concatenate([inner, inner], axis=1)
    lane_r = lax.broadcasted_iota(jnp.int32, (total_tok, 2 * k_in), 1) // k_in
    inner = jnp.where(lane_r == rank_of, inner, 0.0)
    inner_hi = inner.astype(BF16)
    inner_v[:, :2 * k_in] = inner_hi
    inner_v[:, 2 * k_in:] = (inner - inner_hi.astype(F32)).astype(BF16)
    row_b = lax.broadcasted_iota(jnp.int32, (n_store * m_loc, 2 * k_in), 0) // m_loc
    row_r = lax.broadcasted_iota(jnp.int32, (n_store * m_loc, 2 * k_in), 1) // k_in
    held = jnp.zeros((n_store * m_loc, 2 * k_in), jnp.int32)
    for d in dests:
        held = held + (row_b == d).astype(jnp.int32)
    dead_v[...] = jnp.where(row_r < held, 0.0, jnp.nan).astype(F32)

    def wait_recv(ref, kind):
        pltpu.make_async_copy(ref, ref, recv_sem.at[kind]).wait()

    wait_recv(hit_recv.at[0:n_pb - 1], 0)
    hit_sum = hit_recv[0].astype(F32)
    for p in range(1, n_pb):
        hit_sum = hit_sum + hit_recv[p].astype(F32)
    outer = []
    for chunk in range(CHUNKS):
        wait_recv(u_recv.at[chunk, 0:n_pb - 1], 1 + chunk)
        tops = [u_recv[chunk, p, m_loc:m_loc + 1, :] for p in range(n_pb)]
        sums = [u_recv[chunk, p, m_loc + 1:m_loc + 2, :] for p in range(n_pb)]
        top = functools.reduce(jnp.maximum, tops)
        weights = [jnp.exp(t - top) for t in tops]
        total = functools.reduce(jnp.add, [w * s for w, s in zip(weights, sums)])
        acc = functools.reduce(
            jnp.add, [w * u_recv[chunk, p, 0:m_loc, :] for p, w in enumerate(weights)]
        )
        outer.append(acc / total - hit_sum[:, chunk * part_t:(chunk + 1) * part_t])
    outer = jnp.concatenate(outer, axis=1)

    outer_hi = outer.astype(BF16)
    outer_lo = (outer - outer_hi.astype(F32)).astype(BF16)
    mask = mask_v[...].reshape(n_store, m_loc, total_tok)
    placed_hi = (mask * outer_hi[None]).reshape(n_store * m_loc, total_tok)
    placed_lo = (mask * outer_lo[None]).reshape(n_store * m_loc, total_tok)
    both = jnp.dot(placed_hi, inner_v[...], preferred_element_type=F32)
    rest = jnp.dot(placed_lo, inner_v[:, :2 * k_in], preferred_element_type=F32)
    grads = both[:, :2 * k_in] + (both[:, 2 * k_in:] + rest) + dead_v[...]
    g_send[...] = grads.astype(BF16).reshape(g_send.shape)
    g_kind = 2 + CHUNKS

    def g_copy(i):
        peer = store_peer(i)
        return pltpu.make_async_remote_copy(
            src_ref=g_send.at[peer], dst_ref=g_recv.at[me_s],
            send_sem=send_sem.at[g_kind], recv_sem=recv_sem.at[g_kind],
            device_id={"store": peer}, device_id_type=MESH,
        )

    @pl.loop(1, n_store)
    def _(i):
        g_copy(i).start()

    g_recv[me_s] = g_send[me_s]
    wait_recv(q_recv.at[0:n_pb - 1], q_kind)
    lhs = jnp.concatenate(
        [q_recv[:, j].reshape(n_pb * per_query, 2 * k_in) for j in range(half)], axis=1
    )
    wait_recv(g_recv.at[0:n_store - 1], g_kind)

    g_rows[...] = g_recv[...].astype(F32).reshape(g_rows.shape)
    low = lax.broadcasted_iota(jnp.int32, (n_store, 2 * k_in), 1) < k_in
    rhs = []
    for j in range(half):
        first = g_rows[pl.ds(j, n_store, stride=m_loc), :]
        second = g_rows[pl.ds(j + half, n_store, stride=m_loc), :]
        slot0 = jnp.where(low, first, pltpu.roll(second, k_in, 1))
        slot1 = jnp.where(low, pltpu.roll(first, k_in, 1), second)
        rhs.append(jnp.concatenate([slot0, slot1], axis=0))
    rhs = jnp.concatenate(rhs, axis=1).astype(BF16)
    part = lax.dot_general(lhs, rhs, NT, preferred_element_type=F32)
    slots = CAP * n_store
    s_send[...] = part.reshape(n_pb, per_query, slots)
    s_kind = 3 + CHUNKS
    for i in range(1, n_pb):
        copy = pb_copy(i, s_send.at[pb_peer(i)], s_recv.at[me_p], s_kind)
        copy.start()
        sent.append(copy)
    s_recv[me_p] = s_send[me_p]
    wait_recv(s_recv.at[0:n_pb - 1], s_kind)

    scores = s_recv[0]
    for p in range(1, n_pb):
        scores = scores + s_recv[p]
    scores = jnp.where(scores == scores, scores, jnp.float32(-1e30))
    lane = lax.broadcasted_iota(jnp.int32, scores.shape, 1)
    best = jnp.max(scores, axis=1, keepdims=True)
    at = jnp.min(jnp.where(scores == best, lane, slots), axis=1, keepdims=True)
    second = jnp.max(jnp.where(lane == at, jnp.float32(-3e38), scores), axis=1, keepdims=True)
    out[...] = jnp.where(
        lax.broadcasted_iota(jnp.int32, (per_query, K_TOP), 1) == 0, best, second
    )

    for copy in sent:
        copy.wait_send()

    @pl.loop(1, n_store)
    def _(i):
        g_copy(i).wait_send()


def shards(n_store, n_pb, stored_hidden, targets, pick, dest, norm_gain, head, proj_in, proj_out,
           query_grads):
    examples, tokens, width = stored_hidden.shape
    cands = pick.shape[0]
    total = cands * tokens
    v_dev = head.shape[1]
    k_in = proj_in.shape[1]
    m_out = proj_out.shape[1]
    m_loc = m_out // n_pb
    half = m_loc // 2
    per_query = query_grads.shape[0]
    part_t = total // CHUNKS
    wide_n = v_dev + k_in
    slots = CAP * n_store
    any_spec = pl.BlockSpec(memory_space=pl.ANY)
    smem = pl.BlockSpec(memory_space=pltpu.SMEM)
    vmem = pltpu.VMEM
    kinds = 4 + CHUNKS
    return pl.pallas_call(
        functools.partial(kernel, n_store, n_pb),
        out_shape=jax.ShapeDtypeStruct((per_query, K_TOP), F32),
        in_specs=[smem, smem] + [any_spec] * 7,
        out_specs=pl.BlockSpec(memory_space=pltpu.VMEM),
        scratch_shapes=[
            vmem((examples, tokens, width), BF16),
            vmem((examples, tokens), jnp.int32),
            vmem((1, width), F32),
            vmem((width, wide_n), BF16),
            vmem((width, k_in), BF16),
            vmem((v_dev, m_out), BF16),
            vmem((per_query, k_in * m_out), BF16),
            vmem((examples, tokens, width), BF16),
            vmem((total, wide_n), F32),
            vmem((total, 4 * k_in), BF16),
            vmem((n_store * m_loc, total), BF16),
            vmem((n_store * m_loc, 2 * k_in), F32),
            vmem((k_in * per_query, m_out), F32),
            vmem((n_pb * half * per_query, 2 * k_in), F32),
            vmem((n_pb, half, per_query, 2 * k_in), BF16),
            vmem((n_pb, half, per_query, 2 * k_in), BF16),
            vmem((n_pb, m_loc, total), BF16),
            vmem((n_pb, m_loc, total), BF16),
            vmem((CHUNKS, n_pb, m_loc + 8, part_t), F32),
            vmem((CHUNKS, n_pb, m_loc + 8, part_t), F32),
            vmem((n_store, m_loc, 2 * k_in), BF16),
            vmem((n_store, m_loc, 2 * k_in), BF16),
            vmem((n_store * m_loc, 2 * k_in), F32),
            vmem((n_pb, per_query, slots), F32),
            vmem((n_pb, per_query, slots), F32),
            pltpu.SemaphoreType.DMA((5,)),
            pltpu.SemaphoreType.DMA((examples,)),
            pltpu.SemaphoreType.DMA((-(-v_dev // 256),)),
            pltpu.SemaphoreType.DMA((kinds,)),
            pltpu.SemaphoreType.DMA((kinds,)),
        ],
        compiler_params=pltpu.CompilerParams(
            collective_id=0, has_side_effects=True, vmem_limit_bytes=48 * 1024 * 1024
        ),
        name="attribution",
    )(pick, dest, stored_hidden, targets, norm_gain.reshape(1, width), head, proj_in, proj_out,
      query_grads)


def solution(mesh):
    placed = (
        P("store", None, None),
        P("store", None),
        P("store"),
        P("store"),
        P(),
        P(None, "pb"),
        P(),
        P("pb", None),
        P(("store", "pb"), None),
    )
    body = functools.partial(shards, mesh.shape["store"], mesh.shape["pb"])
    return jax.shard_map(
        body, mesh=mesh, in_specs=placed, out_specs=P(("store", "pb"), None), check_vma=False
    )
```

```python
import functools

import jax
import jax.numpy as jnp
from jax import lax
from jax.experimental import pallas as pl
from jax.experimental.pallas import tpu as pltpu
from jax.sharding import PartitionSpec as P

CAP = 2
K_TOP = 2
CHUNKS = 2
STEP = 128
MESH = pl.DeviceIdType.MESH
F32 = jnp.float32
BF16 = jnp.bfloat16
NT = (((1,), (1,)), ((), ()))
TN = (((0,), (0,)), ((), ()))


def ring_hops(i, n):
    y, z = i % 4, i // 4
    return min(y, 4 - y) + max(min(z, n // 4 - z), min(z + 1, n // 4 - z - 1))


def kernel(
    n_store, n_pb,
    pick_h, dest_h, hid, tgt, gain, head, pin, pout, query,
    out,
    pick, dest, hid_v, tgt_v, gain_v, wide_w, pin_v, pout_v, query_v,
    normed, logits, inner_v, mask_v, dead_v, wanted_v,
    q_rows, q_mid, q_send, q_recv,
    hit_send, hit_recv, u_send, u_recv, t_send, t_recv, g_send, g_recv, g_rows, s_send, s_recv,
    load_sem, hid_sem, head_sem, send_sem, recv_sem,
):
    examples, tokens, width = hid.shape
    cands = pick_h.shape[0]
    total_tok = cands * tokens
    v_dev = head.shape[1]
    k_in = pin.shape[0]
    m_out = pout.shape[1]
    m_loc = m_out // n_pb
    half = m_loc // 2
    per_query = query.shape[0]
    me_s = lax.axis_index("store")
    me_p = lax.axis_index("pb")

    def pb_peer(i):
        return lax.rem(me_p + i, n_pb)

    far_pb = sorted(range(1, n_pb), key=lambda i: abs(i - n_pb // 2))

    def store_peer(i):
        return lax.rem(me_s + i, n_store)

    small = [
        pltpu.make_async_copy(src, dst, load_sem.at[i])
        for i, (src, dst) in enumerate(
            [(gain, gain_v), (tgt, tgt_v), (pout, pout_v), (pin, pin_v), (query, query_v),
             (pick_h, pick), (dest_h, dest)]
        )
    ]
    gain_load, tgt_load, pout_load, pin_load, query_load, pick_load, dest_load = small
    cuts = list(range(0, v_dev, 256)) + [v_dev]
    head_loads = [
        pltpu.make_async_copy(
            head.at[:, lo:hi], wide_w.at[:, lo:hi], head_sem.at[i]
        )
        for i, (lo, hi) in enumerate(zip(cuts[:-1], cuts[1:]))
    ]

    def hid_load(e):
        return pltpu.make_async_copy(hid.at[e], hid_v.at[e], hid_sem.at[e])

    for load in (pick_load, dest_load, tgt_load, pout_load, pin_load, gain_load):
        load.start()

    @pl.loop(0, examples)
    def _(e):
        hid_load(e).start()

    head_loads[0].start()

    barrier = pltpu.get_barrier_semaphore()
    for i in range(1, n_pb):
        pl.semaphore_signal(barrier, inc=1, device_id={"pb": pb_peer(i)}, device_id_type=MESH)

    @pl.loop(1, n_store)
    def _(i):
        pl.semaphore_signal(
            barrier, inc=1, device_id={"store": store_peer(i)}, device_id_type=MESH
        )

    for load in (pick_load, dest_load, tgt_load, pout_load, pin_load, gain_load):
        load.wait()
    picks = [pick[c] for c in range(cands)]
    wanted = jnp.concatenate([tgt_v[pl.ds(p, 1), :] for p in picks], axis=1) - me_p * v_dev
    column = lax.broadcasted_iota(jnp.int32, (v_dev, total_tok), 0)
    hit = jnp.where(column == wanted, 1.0, 0.0).astype(BF16)
    hit_rows = lax.dot_general(pout_v[...], hit, TN, preferred_element_type=F32)
    hit_send[...] = hit_rows.astype(BF16).reshape(n_pb, m_loc, total_tok)
    wanted_v[...] = jnp.broadcast_to(wanted.astype(F32), (128, total_tok)).T
    wide_w[:, v_dev:v_dev + k_in] = pin_v[...].T

    def pb_copy(i, src, dst, kind):
        return pltpu.make_async_remote_copy(
            src_ref=src, dst_ref=dst, send_sem=send_sem.at[kind], recv_sem=recv_sem.at[kind],
            device_id={"pb": pb_peer(i)}, device_id_type=MESH,
        )

    def hid_wait(lo, hi):
        pl.loop(lo, hi)(lambda e: hid_load(e).wait())

    hid_wait(0, examples)
    for load in head_loads[1:]:
        load.start()
    query_load.start()

    rows = 16
    step = STEP

    def normalise(lo):
        for t in range(lo, lo + step, rows):
            p, r = picks[t // tokens], t % tokens
            square = jnp.zeros((rows, 128), F32)
            for c in range(0, width, 128):
                wide = hid_v[p, r:r + rows, c:c + 128].astype(F32)
                square = square + wide * wide
            mean = jnp.sum(square, axis=1, keepdims=True) * (1.0 / width)
            scale = jnp.broadcast_to(lax.rsqrt(mean + 1e-05), (rows, 128))
            for c in range(0, width, 128):
                wide = hid_v[p, r:r + rows, c:c + 128].astype(F32)
                normed[t:t + rows, c:c + 128] = (wide * scale * gain_v[:, c:c + 128]).astype(BF16)

    def multiply(lo, n):
        c0, c1 = cuts[n], cuts[n + 1]
        logits[lo:lo + step, c0:c1] = jnp.dot(
            normed[lo:lo + step, :], wide_w[:, c0:c1], preferred_element_type=F32
        )

    cuts = cuts[:-1] + [v_dev + k_in]
    last = len(cuts) - 2
    normalise(0)
    for n in range(last):
        head_loads[n].wait()
        if n == last - 1:
            pl.semaphore_wait(barrier, n_pb - 1 + n_store - 1)
            for i in far_pb:
                copy = pb_copy(i, hit_send.at[pb_peer(i)], hit_recv.at[me_p], 0)
                copy.start()
            hit_recv[me_p] = hit_send[me_p]
        for lo in range(0, total_tok, step):
            multiply(lo, n)
            if n == 0 and lo + step < total_tok:
                normalise(lo + step)
    head_loads[last].wait()
    for lo in range(0, total_tok, step):
        multiply(lo, last)

    part_t = total_tok // CHUNKS
    subs = part_t // step
    lane = lax.broadcasted_iota(jnp.int32, (step, 128), 1)
    entry = lax.broadcasted_iota(jnp.int32, (step, v_dev), 1).astype(F32)
    t_send[...] = jnp.zeros(t_send.shape, F32)
    for chunk in range(CHUNKS):
        for sub in range(subs):
            lo = chunk * part_t + sub * step
            local = logits[lo:lo + step, :v_dev]
            top = jnp.max(local, axis=1, keepdims=True)
            expo = jnp.exp(local - top)
            target = jnp.concatenate([wanted_v[lo:lo + step, :]] * (v_dev // 128), axis=1)
            is_hit = entry == target
            others = jnp.where(is_hit, 0.0, expo)
            total = jnp.sum(others, axis=1, keepdims=True)
            own = jnp.sum(jnp.where(is_hit, expo, 0.0), axis=1, keepdims=True)
            part = jnp.dot(others.astype(BF16), pout_v[...], preferred_element_type=F32)
            stats = jnp.where(lane == 0, top, jnp.where(lane == 1, total, own)).T
            for row in range(3):
                t_send[chunk, row * subs + sub:row * subs + sub + 1, :] = stats[row:row + 1]
            u_send[chunk, :, :, sub * step:(sub + 1) * step] = part.T.astype(BF16).reshape(
                n_pb, m_loc, step
            )
        for i in far_pb:
            copy = pb_copy(i, u_send.at[chunk, pb_peer(i)], u_recv.at[chunk, me_p], 1 + 2 * chunk)
            copy.start()
            copy = pb_copy(i, t_send.at[chunk], t_recv.at[chunk, me_p], 2 + 2 * chunk)
            copy.start()
        u_recv[chunk, me_p] = u_send[chunk, me_p]
        t_recv[chunk, me_p] = t_send[chunk]

    query_load.wait()
    for k in range(k_in):
        q_rows[k * per_query:(k + 1) * per_query, :] = query_v[
            :, k * m_out:(k + 1) * m_out
        ].astype(F32)
    low = lax.broadcasted_iota(jnp.int32, (half, 2 * k_in), 1) < k_in
    for q in range(per_query):
        square = q_rows[pl.ds(q, k_in, stride=per_query), :]
        turned = jnp.concatenate([square, square], axis=0).T
        for p in range(n_pb):
            first = turned[p * m_loc:p * m_loc + half]
            second = turned[p * m_loc + half:(p + 1) * m_loc]
            q_mid[pl.ds(p * half * per_query + q, half, stride=per_query), :] = jnp.where(
                low, first, second
            )
    q_send[...] = q_mid[...].astype(BF16).reshape(q_send.shape)
    q_kind = 1 + 2 * CHUNKS
    q_recv[me_p] = q_send[me_p]

    dests = [dest[c] for c in range(cands)]
    ranks = []
    for c in range(cands):
        rank = jnp.int32(0)
        for d in dests[:c]:
            rank = rank + (d == dests[c]).astype(jnp.int32)
        ranks.append(rank)
    block_of = jnp.concatenate(
        [jnp.full((1, tokens), d, jnp.int32) for d in dests], axis=1
    )
    grid_b = lax.broadcasted_iota(jnp.int32, (n_store * m_loc, total_tok), 0) // m_loc
    mask_v[...] = jnp.where(grid_b == block_of, 1.0, 0.0).astype(BF16)
    rank_of = jnp.concatenate([jnp.full((tokens, 2 * k_in), r, jnp.int32) for r in ranks], axis=0)
    inner = logits[:, v_dev:v_dev + k_in]
    inner = jnp.concatenate([inner, inner], axis=1)
    lane_r = lax.broadcasted_iota(jnp.int32, (total_tok, 2 * k_in), 1) // k_in
    inner = jnp.where(lane_r == rank_of, inner, 0.0)
    inner_hi = inner.astype(BF16)
    inner_v[:, :2 * k_in] = inner_hi
    inner_v[:, 2 * k_in:] = (inner - inner_hi.astype(F32)).astype(BF16)
    row_b = lax.broadcasted_iota(jnp.int32, (n_store * m_loc, 2 * k_in), 0) // m_loc
    row_r = lax.broadcasted_iota(jnp.int32, (n_store * m_loc, 2 * k_in), 1) // k_in
    held = jnp.zeros((n_store * m_loc, 2 * k_in), jnp.int32)
    for d in dests:
        held = held + (row_b == d).astype(jnp.int32)
    dead_v[...] = jnp.where(row_r < held, 0.0, jnp.nan).astype(F32)

    def wait_recv(ref, kind):
        pltpu.make_async_copy(ref, ref, recv_sem.at[kind]).wait()

    def wait_send(ref, kind):
        pltpu.make_async_copy(ref, ref, send_sem.at[kind]).wait()

    wait_recv(hit_recv.at[0:n_pb - 1], 0)
    hit_sum = hit_recv[0].astype(F32)
    for p in range(1, n_pb):
        hit_sum = hit_sum + hit_recv[p].astype(F32)
    for chunk in range(CHUNKS):
        wait_recv(u_recv.at[chunk, 0:n_pb - 1], 1 + 2 * chunk)
        wait_recv(t_recv.at[chunk, 0:n_pb - 1], 2 + 2 * chunk)
    for i in far_pb:
        copy = pb_copy(i, q_send.at[pb_peer(i)], q_recv.at[me_p], q_kind)
        copy.start()
    outer = []
    for chunk in range(CHUNKS):
        for sub in range(subs):
            tops, totals, owns = (
                [t_recv[chunk, p, row * subs + sub:row * subs + sub + 1, :] for p in range(n_pb)]
                for row in range(3)
            )
            top = functools.reduce(jnp.maximum, tops)
            weights = [jnp.exp(t - top) for t in tops]
            others = functools.reduce(jnp.add, [w * t for w, t in zip(weights, totals)])
            total = others + functools.reduce(jnp.add, [w * o for w, o in zip(weights, owns)])
            acc = functools.reduce(jnp.add, [
                w * u_recv[chunk, p, :, sub * step:(sub + 1) * step].astype(F32)
                for p, w in enumerate(weights)
            ])
            lo = chunk * part_t + sub * step
            outer.append((acc - others * hit_sum[:, lo:lo + step]) / total)
    outer = jnp.concatenate(outer, axis=1)

    outer_hi = outer.astype(BF16)
    outer_lo = (outer - outer_hi.astype(F32)).astype(BF16)
    mask = mask_v[...].reshape(n_store, m_loc, total_tok)
    placed_hi = (mask * outer_hi[None]).reshape(n_store * m_loc, total_tok)
    placed_lo = (mask * outer_lo[None]).reshape(n_store * m_loc, total_tok)
    both = jnp.dot(placed_hi, inner_v[...], preferred_element_type=F32)
    rest = jnp.dot(placed_lo, inner_v[:, :2 * k_in], preferred_element_type=F32)
    grads = both[:, :2 * k_in] + (both[:, 2 * k_in:] + rest) + dead_v[...]
    g_send[...] = grads.astype(BF16).reshape(g_send.shape)
    g_kind = 2 + 2 * CHUNKS

    far = sorted(range(1, n_store), key=lambda i: -ring_hops(i, n_store))
    for i in far:
        peer = store_peer(i)
        copy = pltpu.make_async_remote_copy(
            src_ref=g_send.at[peer], dst_ref=g_recv.at[me_s],
            send_sem=send_sem.at[g_kind], recv_sem=recv_sem.at[g_kind],
            device_id={"store": peer}, device_id_type=MESH,
        )
        copy.start()
    g_recv[me_s] = g_send[me_s]
    wait_recv(q_recv.at[0:n_pb - 1], q_kind)
    lhs = jnp.concatenate(
        [q_recv[:, j].reshape(n_pb * per_query, 2 * k_in) for j in range(half)], axis=1
    )
    wait_send(hit_send.at[0:n_pb - 1], 0)
    for chunk in range(CHUNKS):
        wait_send(u_send.at[chunk, 0:n_pb - 1], 1 + 2 * chunk)
        wait_send(t_recv.at[chunk, 0:n_pb - 1], 2 + 2 * chunk)
    wait_send(q_send.at[0:n_pb - 1], q_kind)
    wait_recv(g_recv.at[0:n_store - 1], g_kind)

    g_rows[...] = g_recv[...].astype(F32).reshape(g_rows.shape)
    low = lax.broadcasted_iota(jnp.int32, (n_store, 2 * k_in), 1) < k_in
    rhs = []
    for j in range(half):
        first = g_rows[pl.ds(j, n_store, stride=m_loc), :]
        second = g_rows[pl.ds(j + half, n_store, stride=m_loc), :]
        slot0 = jnp.where(low, first, pltpu.roll(second, k_in, 1))
        slot1 = jnp.where(low, pltpu.roll(first, k_in, 1), second)
        rhs.append(jnp.concatenate([slot0, slot1], axis=0))
    rhs = jnp.concatenate(rhs, axis=1).astype(BF16)
    part = lax.dot_general(lhs, rhs, NT, preferred_element_type=F32)
    slots = CAP * n_store
    s_send[...] = part.reshape(n_pb, per_query, slots)
    s_kind = 3 + 2 * CHUNKS
    for i in far_pb:
        copy = pb_copy(i, s_send.at[pb_peer(i)], s_recv.at[me_p], s_kind)
        copy.start()
    s_recv[me_p] = s_send[me_p]
    wait_send(g_send.at[0:n_store - 1], g_kind)
    wait_recv(s_recv.at[0:n_pb - 1], s_kind)

    scores = s_recv[0]
    for p in range(1, n_pb):
        scores = scores + s_recv[p]
    scores = jnp.where(scores == scores, scores, jnp.float32(-1e30))
    lane = lax.broadcasted_iota(jnp.int32, scores.shape, 1)
    best = jnp.max(scores, axis=1, keepdims=True)
    at = jnp.min(jnp.where(scores == best, lane, slots), axis=1, keepdims=True)
    second = jnp.max(jnp.where(lane == at, jnp.float32(-3e38), scores), axis=1, keepdims=True)
    both = jnp.where(lax.broadcasted_iota(jnp.int32, (per_query, 128), 1) == 0, best, second)
    out[...] = both.T[0:K_TOP]

    wait_send(s_send.at[0:n_pb - 1], s_kind)


def shards(n_store, n_pb, stored_hidden, targets, pick, dest, norm_gain, head, proj_in, proj_out,
           query_grads):
    examples, tokens, width = stored_hidden.shape
    cands = pick.shape[0]
    total = cands * tokens
    v_dev = head.shape[1]
    k_in = proj_in.shape[1]
    m_out = proj_out.shape[1]
    m_loc = m_out // n_pb
    half = m_loc // 2
    per_query = query_grads.shape[0]
    part_t = total // CHUNKS
    wide_n = v_dev + k_in
    slots = CAP * n_store
    any_spec = pl.BlockSpec(memory_space=pl.ANY)
    vmem = pltpu.VMEM
    kinds = 4 + 2 * CHUNKS
    return pl.pallas_call(
        functools.partial(kernel, n_store, n_pb),
        out_shape=jax.ShapeDtypeStruct((K_TOP, per_query), F32),
        in_specs=[any_spec] * 9,
        out_specs=pl.BlockSpec(memory_space=pltpu.VMEM),
        scratch_shapes=[
            pltpu.SMEM((cands,), jnp.int32),
            pltpu.SMEM((cands,), jnp.int32),
            vmem((examples, tokens, width), BF16),
            vmem((examples, tokens), jnp.int32),
            vmem((1, width), F32),
            vmem((width, wide_n), BF16),
            vmem((k_in, width), BF16),
            vmem((v_dev, m_out), BF16),
            vmem((per_query, k_in * m_out), BF16),
            vmem((total, width), BF16),
            vmem((total, wide_n), F32),
            vmem((total, 4 * k_in), BF16),
            vmem((n_store * m_loc, total), BF16),
            vmem((n_store * m_loc, 2 * k_in), F32),
            vmem((total, 128), F32),
            vmem((k_in * per_query, m_out), F32),
            vmem((n_pb * half * per_query, 2 * k_in), F32),
            vmem((n_pb, half, per_query, 2 * k_in), BF16),
            vmem((n_pb, half, per_query, 2 * k_in), BF16),
            vmem((n_pb, m_loc, total), BF16),
            vmem((n_pb, m_loc, total), BF16),
            vmem((CHUNKS, n_pb, m_loc, part_t), BF16),
            vmem((CHUNKS, n_pb, m_loc, part_t), BF16),
            vmem((CHUNKS, 8, 128), F32),
            vmem((CHUNKS, n_pb, 8, 128), F32),
            vmem((n_store, m_loc, 2 * k_in), BF16),
            vmem((n_store, m_loc, 2 * k_in), BF16),
            vmem((n_store * m_loc, 2 * k_in), F32),
            vmem((n_pb, per_query, slots), F32),
            vmem((n_pb, per_query, slots), F32),
            pltpu.SemaphoreType.DMA((7,)),
            pltpu.SemaphoreType.DMA((examples,)),
            pltpu.SemaphoreType.DMA((-(-v_dev // 256),)),
            pltpu.SemaphoreType.DMA((kinds,)),
            pltpu.SemaphoreType.DMA((kinds,)),
        ],
        compiler_params=pltpu.CompilerParams(
            collective_id=0, has_side_effects=True, vmem_limit_bytes=63 * 1024 * 1024
        ),
        name="attribution",
    )(pick, dest, stored_hidden, targets, norm_gain.reshape(1, width), head, proj_in.T, proj_out,
      query_grads).T


def solution(mesh):
    placed = (
        P("store", None, None),
        P("store", None),
        P("store"),
        P("store"),
        P(),
        P(None, "pb"),
        P(),
        P("pb", None),
        P(("store", "pb"), None),
    )
    body = functools.partial(shards, mesh.shape["store"], mesh.shape["pb"])
    return jax.shard_map(
        body, mesh=mesh, in_specs=placed, out_specs=P(("store", "pb"), None), check_vma=False
    )
```
